32 devices in a mesh: seq: 4 (over z), head: 8 (over y, x, core).
Axes of the slice: x: 2, y: 2, z: 4, core: 2. Of those that a mesh axis runs over, the one named last changes fastest.
Arguments:
- tokens: bfloat16 [512, 4096], P('seq', 'head'), may hold values from -24 to 24
- query_weight: bfloat16 [4096, 4096], P('head'), may hold values from -3 to 3
- key_weight: bfloat16 [1024, 4096], P('head'), may hold values from -3 to 3
- value_weight: bfloat16 [1024, 4096], P('head'), may hold values from -0.09375 to 0.09375
- output_weight: bfloat16 [4096, 4096], P('head'), may hold values from -0.5 to 0.5
- segments: int32 [512], replicated, may hold values from 0 to 7, never falling along the last dimension, each value on 1 to 384 neighbouring positions
Outputs:
- attention_out: bfloat16 [512, 4096], P('seq', 'head')
The draws below stay inside these ranges and needn't reach their ends.
All inputs are finite; a program needn't handle non-finite values.
Results may differ from the reference program's by a relative error of at most 0.011.
Values may be sent and summed in bfloat16 or wider, within the bound.
A program may use at most 64 MiB of HBM per device.

```python
import math
import jax
import jax.numpy as jnp
import numpy as np
from jax import lax

D = 4096
HEADS = 32
KV_HEADS = 8
HEAD_DIM = 128
TOKENS = 512
DOCS = 8
LONGEST = 384


def draw_tokens(key, part):
    sample = jax.random.normal(jax.random.fold_in(key, 204), (TOKENS, D), jnp.float32)
    return jnp.clip(sample, -6.0, 6.0).astype(jnp.bfloat16)


def draw_query_weight(key, part):
    sample = jax.random.normal(jax.random.fold_in(key, 303), (D, HEADS * HEAD_DIM), jnp.float32)
    return (jnp.clip(sample, -6.0, 6.0) / math.sqrt(D)).T.astype(jnp.bfloat16)


def draw_key_weight(key, part):
    sample = jax.random.normal(jax.random.fold_in(key, 401), (D, KV_HEADS * HEAD_DIM), jnp.float32)
    return (jnp.clip(sample, -6.0, 6.0) / math.sqrt(D)).T.astype(jnp.bfloat16)


def strengthened(entries, key, source, target, blocks, factor):
    def block_of(axis_at):
        return (jnp.arange(entries.shape[axis_at]) // (entries.shape[axis_at] // blocks)).reshape((-1,) + (1,) * (entries.ndim - 1 - axis_at))

    first = jax.random.permutation(key, blocks)[block_of(target)]
    other_side = (block_of(target) + blocks // 2) % blocks
    return jnp.where((block_of(source) == first) | (block_of(source) == other_side), factor * entries, entries)


def steps_of(stream_key, shape, cuts, least, largest):
    gain = 1.0
    for dim, shards_of in cuts:
        heights = jax.random.uniform(jax.random.fold_in(jax.random.fold_in(stream_key, 6), dim), (shards_of,), jnp.float32, least / len(cuts), largest / len(cuts))
        gain = gain * jnp.repeat(jnp.exp(heights), shape[dim] // shards_of).reshape((-1,) + (1,) * (len(shape) - 1 - dim))
    return gain


def length_profile(amount, total, limit, lean):
    portions = [(1 << 20) // math.isqrt(grade ** lean) + 1 for grade in range(2, amount + 1)]
    surplus, counts = total - limit - (amount - 1), [1] * (amount - 1)
    while surplus > 0:
        candidates = [i for i in range(amount - 1) if counts[i] < limit]
        mass, left = sum([portions[i] for i in candidates]), surplus
        for i in candidates:
            addition = min(limit - counts[i], max(1, left * portions[i] // mass), surplus)
            counts[i] = counts[i] + addition
            surplus = surplus - addition
    return np.array([limit] + counts)


def uneven(stream_key, amount, total, bound, skew):
    if amount == 2:
        one = jax.random.randint(stream_key, (), max(1, total - bound), min(bound, total - 1) + 1)
        return jnp.stack([one, total - one])
    lengths = jnp.asarray(length_profile(amount, total, bound, skew), jnp.int32)
    pairs = (amount - 1) // 2
    donor, sink = lengths[1:1 + 2 * pairs:2], lengths[2:2 + 2 * pairs:2]
    room = jnp.minimum(donor - 1, bound - sink)
    moved = jax.random.randint(jax.random.fold_in(stream_key, 1), (pairs,), 0, 1 << 20) % (room + 1)
    lengths = lengths.at[1:1 + 2 * pairs:2].set(donor - moved).at[2:2 + 2 * pairs:2].set(sink + moved)
    return lengths[jax.random.permutation(jax.random.fold_in(stream_key, 2), amount)]


def bell_draw(key, dims, scale, reach, split=(), kind=jnp.bfloat16):
    drawn = jax.random.normal(key, dims, jnp.float32) * scale
    if len(split) > 0:
        drawn = steps_of(key, dims, split, -0.22, 0.18) * drawn
    return jnp.clip(drawn, min=-reach, max=reach).astype(kind)


def gaussian_with(stream_key, extent, scale, bound, shards, heavy, held_as=jnp.bfloat16):
    values = scale * jax.random.normal(stream_key, extent, jnp.float32)
    if shards:
        values = values * steps_of(stream_key, extent, shards, -0.22, 0.18)
    return jnp.clip(strengthened(values, jax.random.fold_in(stream_key, 3), *heavy), -bound, bound).astype(held_as)


def setup_inputs(seed: int = 0) -> dict:
    arg_keys = jax.random.split(jax.random.key(seed), 7)
    return {
        "tokens": draw_tokens(jax.random.fold_in(arg_keys[6], 71), 0),
        "query_weight": draw_query_weight(jax.random.fold_in(arg_keys[6], 71), 0),
        "key_weight": draw_key_weight(jax.random.fold_in(arg_keys[6], 71), 0),
        "value_weight": bell_draw(arg_keys[3], (KV_HEADS * HEAD_DIM, D), D ** -0.5, 0.09375, ((0, 8),)),
        "output_weight": gaussian_with(arg_keys[4], (HEADS * HEAD_DIM, D), (HEADS * HEAD_DIM // 16) ** -0.5, 0.5, ((0, 8),), (0, 1, 8, 2.0)),
        "segments": jnp.searchsorted(jnp.cumsum(uneven(arg_keys[5], DOCS, TOKENS, LONGEST, 0)), jnp.arange(TOKENS), side="right").astype(jnp.int32),
    }


def reference(tokens, query_weight, key_weight, value_weight, output_weight, segments):
    queries = jnp.dot(tokens, query_weight.T, preferred_element_type=jnp.float32).astype(jnp.bfloat16)
    keys = jnp.dot(tokens, key_weight.T, preferred_element_type=jnp.float32).astype(jnp.bfloat16)
    values = jnp.dot(tokens, value_weight.T, preferred_element_type=jnp.float32).astype(jnp.bfloat16)
    position = jnp.arange(TOKENS, dtype=jnp.int32)
    allowed = (segments[:, None] == segments[None, :]) & (position[None, :] <= position[:, None])
    scale = 1.0 / math.sqrt(HEAD_DIM)
    per_shared = HEADS // KV_HEADS

    def one_head(head):
        query_head = lax.dynamic_slice_in_dim(queries, (head * HEAD_DIM).astype(jnp.int32), HEAD_DIM, 1)
        shared = (head // per_shared * HEAD_DIM).astype(jnp.int32)
        key_head = lax.dynamic_slice_in_dim(keys, shared, HEAD_DIM, 1)
        value_head = lax.dynamic_slice_in_dim(values, shared, HEAD_DIM, 1)
        scores = jnp.dot(query_head, key_head.T, preferred_element_type=jnp.float32) * scale
        scores = jnp.where(allowed, scores, -1e+30)
        highest = lax.optimization_barrier(jnp.max(scores, axis=1, keepdims=True))
        powers = jnp.where(allowed, jnp.exp(scores - highest), 0.0)
        totals = lax.optimization_barrier(jnp.sum(powers, axis=1, keepdims=True))
        mixed = jnp.dot(powers.astype(jnp.bfloat16), value_head, preferred_element_type=jnp.float32) / totals
        return mixed.astype(jnp.bfloat16)
    stacked = lax.map(one_head, jnp.arange(HEADS, dtype=jnp.int32))
    attended = jnp.transpose(stacked, (1, 0, 2)).reshape(TOKENS, HEADS * HEAD_DIM)
    width = 2 * HEAD_DIM

    def add_pair(total, index):
        start = (index * width).astype(jnp.int32)
        columns = lax.dynamic_slice_in_dim(attended, start, width, 1)
        weight_rows = lax.dynamic_slice_in_dim(output_weight, start, width, 0)
        part = jnp.dot(columns, weight_rows, preferred_element_type=jnp.float32).astype(jnp.bfloat16)
        part = lax.optimization_barrier(part)
        return (total + part.astype(jnp.float32), None)
    summed, unused = lax.scan(add_pair, jnp.zeros((TOKENS, D), jnp.float32), jnp.arange(HEADS // 2, dtype=jnp.int32))
    return summed.astype(jnp.bfloat16)
```

```python
import functools
import math

import jax
import jax.numpy as jnp
from jax import lax
from jax.experimental import pallas as pl
from jax.experimental.pallas import tpu as pltpu
from jax.sharding import PartitionSpec as P

HEADS = 32
KV_HEADS = 8
HEAD_DIM = 128
BLOCK = 128
NT = (((1,), (1,)), ((), ()))
NN = (((1,), (0,)), ((), ()))


def dot(a, b, dims):
    return lax.dot_general(a, b, dims, preferred_element_type=jnp.float32)


def fused_kernel(
    n_seq, n_head, x_hbm, wq_hbm, wk_hbm, wv_hbm, wo_hbm, seg, out,
    xs, w, wo, acc, qs, kv, high, total, mixed, att, away, arrived, kept, sent, landed,
    x_sem, w_sem, wo_sem, x_send, x_fwd, x_recv, kv_send, kv_recv,
    core_send, core_recv, chip_send, chip_recv,
):
    s = lax.axis_index("seq")
    h = lax.axis_index("head")
    chips = n_head // 2
    rows, cols = x_hbm.shape
    q_rows = wq_hbm.shape[0]
    dim = wk_hbm.shape[0]
    heads = q_rows // dim
    scale = 1.0 / math.sqrt(dim)

    def flipped(index):
        return index + 1 - 2 * (index % 2)

    def peer(d):
        index, bit = h, 2
        while bit < n_head:
            if 2 * d & bit:
                index = index + bit - 2 * bit * (index // bit % 2)
            bit *= 2
        return index

    def columns(owner):
        return pl.ds(pl.multiple_of(owner * cols, cols), cols)

    other = flipped(h)

    own_x = pltpu.make_async_copy(x_hbm, xs.at[h], x_sem)
    own_x.start()
    owners = []
    for d in range(chips):
        owners += [peer(d), flipped(peer(d))]
    loads = []
    for i, owner in enumerate(owners):
        chunk = []
        for j, (ref, first) in enumerate(((wk_hbm, 0), (wv_hbm, dim), (wq_hbm, 2 * dim))):
            copy = pltpu.make_async_copy(
                ref.at[:, columns(owner)],
                w.at[pl.ds(first, ref.shape[0]), columns(owner)],
                w_sem.at[i, j],
            )
            copy.start()
            chunk.append(copy)
        loads.append(chunk)
    load_wo = pltpu.make_async_copy(wo_hbm, wo, wo_sem)
    load_wo.start()

    barrier = pltpu.get_barrier_semaphore()
    for d in range(1, chips):
        pl.semaphore_signal(barrier, inc=1, device_id={"head": peer(d)})
    pl.semaphore_signal(barrier, inc=1, device_id={"head": other})
    for j in range(1, n_seq):
        pl.semaphore_signal(barrier, inc=1, device_id={"seq": (s + j) % n_seq})
    pl.semaphore_wait(barrier, chips + n_seq - 1)

    def x_copy(source, owner, send_sem, to):
        return pltpu.make_async_remote_copy(
            src_ref=source, dst_ref=xs.at[owner], send_sem=send_sem,
            recv_sem=x_recv.at[owner], device_id={"head": to},
        )

    sends = [x_copy(x_hbm, h, x_send.at[d], peer(d)) for d in range(chips - 1, 0, -1)]
    sends.append(x_copy(x_hbm, h, x_send.at[0], other))
    for copy in sends:
        copy.start()

    def multiply(i, part):
        owner = owners[i]
        product = dot(xs[owner], w[part, columns(owner)], NT)
        if i == 0:
            acc[:, part] = product
        else:
            acc[:, part] += product

    whole = slice(0, 2 * dim + q_rows)
    memory = slice(0, 2 * dim)
    heads_part = slice(2 * dim, 2 * dim + q_rows)
    last = len(owners) - 1
    for i, owner in enumerate(owners):
        if i == 0:
            own_x.wait()
        else:
            x_copy(xs.at[owner], owner, x_send.at[0], other).wait_recv()
        if i > 0 and i % 2 == 0:
            forward = x_copy(xs.at[owner], owner, x_fwd.at[i // 2], other)
            forward.start()
            sends.append(forward)
        for copy in loads[i]:
            copy.wait()
        if i < last:
            multiply(i, whole)
    multiply(last, memory)
    kv[s] = acc[:, memory].astype(jnp.bfloat16)

    def kv_copy(section, slot, to):
        return pltpu.make_async_remote_copy(
            src_ref=kv.at[section], dst_ref=kv.at[section], send_sem=kv_send.at[slot],
            recv_sem=kv_recv.at[section], device_id={"seq": to},
        )

    for j in range(n_seq - 1, 0, -1):
        @pl.when(s + j < n_seq)
        def _():
            kv_copy(s, j, s + j).start()

    multiply(last, heads_part)
    for g in range(heads):
        qs[g * rows:(g + 1) * rows, :] = acc[:, (2 + g) * dim:(3 + g) * dim].astype(jnp.bfloat16)

    def section_segments(section):
        line = seg[:, pl.ds(pl.multiple_of(section * rows, rows), rows)]
        return jnp.broadcast_to(line, (rows, rows))

    row_segment = section_segments(s).T

    def section_scores(section, allowed):
        scores = dot(qs[...], kv[section, :, :dim], NT) * scale
        return jnp.where(jnp.concatenate([allowed] * heads, 0), scores, -1e30)

    def weighted(section, powers):
        return dot(powers.astype(jnp.bfloat16), kv[section, :, dim:], NN)

    at_row = lax.broadcasted_iota(jnp.int32, (rows, rows), 0)
    at_col = lax.broadcasted_iota(jnp.int32, (rows, rows), 1)
    scores = section_scores(s, (row_segment == section_segments(s)) & (at_col <= at_row))
    first_high = jnp.max(scores, axis=1, keepdims=True)
    powers = jnp.exp(scores - first_high)
    high[...] = first_high
    total[...] = jnp.sum(powers, axis=1, keepdims=True)
    mixed[...] = weighted(s, powers)

    for j in range(1, n_seq):
        @pl.when(s >= j)
        def _():
            section = s - j
            kv_copy(section, 0, (s + 1) % n_seq).wait_recv()
            scores = section_scores(section, row_segment == section_segments(section))
            old = high[...]
            new = jnp.maximum(old, jnp.max(scores, axis=1, keepdims=True))
            shrink = jnp.exp(old - new)
            powers = jnp.exp(scores - new)
            high[...] = new
            total[...] = total[...] * shrink + jnp.sum(powers, axis=1, keepdims=True)
            mixed[...] = mixed[...] * shrink + weighted(section, powers)

    for g in range(heads):
        part = slice(g * rows, (g + 1) * rows)
        att[:, g * dim:(g + 1) * dim] = (mixed[part, :] / total[part, :]).astype(jnp.bfloat16)

    load_wo.wait()

    def core_copy(d):
        return pltpu.make_async_remote_copy(
            src_ref=away.at[d], dst_ref=arrived.at[d], send_sem=core_send.at[d],
            recv_sem=core_recv.at[d], device_id={"head": other},
        )

    def chip_copy(d):
        return pltpu.make_async_remote_copy(
            src_ref=sent.at[d], dst_ref=landed.at[d], send_sem=chip_send.at[d],
            recv_sem=chip_recv.at[d], device_id={"head": peer(d)},
        )

    def pass_on(d):
        core_copy(d).wait_recv()
        sent[d] = (kept[d] + arrived[d].astype(jnp.float32)).astype(jnp.bfloat16)
        copy = chip_copy(d)
        copy.start()
        sends.append(copy)

    for d in range(chips - 1, -1, -1):
        away[d] = dot(att[...], wo[:, columns(flipped(peer(d)))], NN).astype(jnp.bfloat16)
        copy = core_copy(d)
        copy.start()
        sends.append(copy)
        kept[d] = dot(att[...], wo[:, columns(peer(d))], NN)
        if d < chips - 1:
            pass_on(d + 1)
    core_copy(0).wait_recv()
    result = kept[0] + arrived[0].astype(jnp.float32)
    for d in range(1, chips):
        chip_copy(d).wait_recv()
        result = result + landed[d].astype(jnp.float32)
    out[...] = result.astype(jnp.bfloat16)

    for copy in sends:
        copy.wait_send()
    for j in range(1, n_seq):
        @pl.when(s + j < n_seq)
        def _():
            kv_copy(s, j, s + j).wait_send()


def fused(tokens, query_weight, key_weight, value_weight, output_weight, segments):
    n_seq, n_head = lax.axis_size("seq"), lax.axis_size("head")
    rows, cols = tokens.shape
    chips = n_head // 2
    q_rows, width = query_weight.shape
    dim = key_weight.shape[0]
    stacked = q_rows // dim * rows
    bf16, f32 = jnp.bfloat16, jnp.float32
    dma = pltpu.SemaphoreType.DMA
    flops = 2 * rows * width * (2 * q_rows + 2 * dim)
    return pl.pallas_call(
        functools.partial(fused_kernel, n_seq, n_head),
        out_shape=jax.ShapeDtypeStruct((rows, cols), bf16),
        in_specs=[pl.BlockSpec(memory_space=pltpu.HBM)] * 5
        + [pl.BlockSpec(memory_space=pltpu.VMEM)],
        out_specs=pl.BlockSpec(memory_space=pltpu.VMEM),
        scratch_shapes=[
            pltpu.VMEM((n_head, rows, cols), bf16),
            pltpu.VMEM((2 * dim + q_rows, width), bf16),
            pltpu.VMEM(output_weight.shape, bf16),
            pltpu.VMEM((rows, 2 * dim + q_rows), f32),
            pltpu.VMEM((stacked, dim), bf16),
            pltpu.VMEM((n_seq, rows, 2 * dim), bf16),
            pltpu.VMEM((stacked, 1), f32),
            pltpu.VMEM((stacked, 1), f32),
            pltpu.VMEM((stacked, dim), f32),
            pltpu.VMEM((rows, q_rows), bf16),
            pltpu.VMEM((chips, rows, cols), bf16),
            pltpu.VMEM((chips, rows, cols), bf16),
            pltpu.VMEM((chips, rows, cols), f32),
            pltpu.VMEM((chips, rows, cols), bf16),
            pltpu.VMEM((chips, rows, cols), bf16),
            dma, dma((n_head, 3)), dma,
            dma((chips,)), dma((chips,)), dma((n_head,)),
            dma((n_seq,)), dma((n_seq,)),
            dma((chips,)), dma((chips,)), dma((chips,)), dma((chips,)),
        ],
        compiler_params=pltpu.CompilerParams(
            collective_id=0, has_side_effects=True, vmem_limit_bytes=48 * 2**20
        ),
        cost_estimate=pl.CostEstimate(
            flops=flops, bytes_accessed=2 * width * (2 * q_rows + 2 * dim), transcendentals=0
        ),
    )(tokens, query_weight, key_weight, value_weight, output_weight, segments.reshape(1, -1))


def swapped(block, axis, apart):
    count = lax.axis_size(axis)
    route = []
    for low in range(count):
        high = low | 1 << apart
        if high != low and high < count:
            route += [(low, high), (high, low)]
    return lax.ppermute(block, axis, route)


def trade_partner(block, bit):
    return swapped(block, "head", bit)


def collect(block, place, bit_list, dim):
    for bit in bit_list:
        flag = place >> bit & 1
        other = trade_partner(block, bit)
        block = jnp.where(
            flag == 0, jnp.concatenate([block, other], dim), jnp.concatenate([other, block], dim)
        )
    return block


def local(tokens, query_weight, key_weight, value_weight, output_weight, segments):
    n_head = lax.axis_size("head")
    split = max(1, 2 * n_head // HEADS)
    groups = n_head // split
    pair_span = n_head // KV_HEADS
    place = lax.axis_index("head")
    seq_place = lax.axis_index("seq")
    local_rows = tokens.shape[0]
    local_cols = tokens.shape[1]
    section = local_rows // split
    piece = section // groups
    split_bits = list(range(split.bit_length() - 1))
    group_bits = list(range(split.bit_length() - 1, n_head.bit_length() - 1))
    span_bits = list(range(pair_span.bit_length() - 1))
    ordered = (
        tokens.reshape(split, groups, piece, local_cols)
        .transpose(1, 0, 2, 3)
        .reshape(n_head * piece, local_cols)
    )
    arrived = lax.all_to_all(ordered, "head", split_axis=0, concat_axis=1, tiled=True)
    rows_here = collect(arrived, place, group_bits, 0)
    head_rows = collect(jnp.stack([query_weight, output_weight]), place, split_bits, 1)
    pair_rows = collect(jnp.stack([key_weight, value_weight]), place, span_bits, 1)
    queries = lax.dot_general(
        rows_here, head_rows[0], (((1,), (1,)), ((), ())), preferred_element_type=jnp.float32
    ).astype(jnp.bfloat16)
    memory_local = jnp.einsum(
        "khd,rd->khr", pair_rows, rows_here, preferred_element_type=jnp.float32
    ).astype(jnp.bfloat16)
    spread = lax.all_gather(memory_local[:, :, None, :], "seq", axis=2, tiled=True)
    memory_all = collect(spread, place, split_bits, 3).reshape(2, HEAD_DIM, -1)
    head_dim = HEAD_DIM
    heads_here = queries.shape[1] // head_dim
    first_row = seq_place * local_rows + place % split * section
    query_position = first_row + lax.iota(jnp.int32, section)
    query_segment = lax.dynamic_slice_in_dim(segments, first_row, section, 0)
    doc_start = jnp.sum((segments < query_segment[0]).astype(jnp.int32))
    first_tile = doc_start // BLOCK
    last_tile = (first_row + section - 1) // BLOCK
    grouped = queries.reshape(section, 1, heads_here, head_dim)
    scale = 1.0 / math.sqrt(head_dim)
    key_rows = memory_all[0]
    value_rows = memory_all[1]

    def visit_tile(tile, carry):
        highest, totals, accum = carry
        begin = tile * BLOCK
        key_tile = lax.dynamic_slice_in_dim(key_rows, begin, BLOCK, 1).reshape(1, head_dim, BLOCK)
        value_tile = lax.dynamic_slice_in_dim(value_rows, begin, BLOCK, 1).reshape(
            1, head_dim, BLOCK
        )
        key_segment = lax.dynamic_slice_in_dim(segments, begin, BLOCK, 0)
        key_position = begin + lax.iota(jnp.int32, BLOCK)
        allowed = (query_segment[:, None] == key_segment[None, :]) & (
            key_position[None, :] <= query_position[:, None]
        )
        scores = (
            jnp.einsum("rkgd,kdb->kgrb", grouped, key_tile, preferred_element_type=jnp.float32)
            * scale
        )
        scores = jnp.where(allowed, scores, -1e30)
        new_highest = jnp.maximum(highest, jnp.max(scores, axis=3))
        shrink = jnp.exp(highest - new_highest)
        powers = jnp.where(allowed, jnp.exp(scores - new_highest[..., None]), 0.0)
        totals = totals * shrink + jnp.sum(powers, axis=3)
        update = jnp.einsum(
            "kgrb,kdb->kgrd",
            powers.astype(jnp.bfloat16),
            value_tile,
            preferred_element_type=jnp.float32,
        )
        accum = accum * shrink[..., None] + update
        return (new_highest, totals, accum)

    start_high = jnp.full((1, heads_here, section), -1e30, jnp.float32)
    start_total = jnp.zeros((1, heads_here, section), jnp.float32)
    start_accum = jnp.zeros((1, heads_here, section, head_dim), jnp.float32)
    highest, totals, accum = lax.fori_loop(
        first_tile, last_tile + 1, visit_tile, (start_high, start_total, start_accum)
    )
    attended = (
        (accum / totals[..., None])
        .transpose(2, 0, 1, 3)
        .reshape(section, heads_here * head_dim)
        .astype(jnp.bfloat16)
    )
    pairs_here = heads_here // 2
    partial_value = jnp.einsum(
        "rpk,pkd->prd",
        attended.reshape(section, pairs_here, 2 * head_dim),
        head_rows[1].reshape(pairs_here, 2 * head_dim, -1),
        preferred_element_type=jnp.float32,
    ).astype(jnp.bfloat16)
    returned = lax.all_to_all(partial_value, "head", split_axis=2, concat_axis=0, tiled=True)
    summed = (
        returned.astype(jnp.float32)
        .reshape(groups, split, pairs_here, section, -1)
        .sum(axis=(0, 2))
    )
    return summed.reshape(split * section, -1).astype(jnp.bfloat16)


def solution(mesh):
    placed = (
        P("seq", "head"),
        P("head", None),
        P("head", None),
        P("head", None),
        P("head", None),
        P(),
    )
    one_head_each = mesh.shape["head"] == KV_HEADS
    return jax.shard_map(
        fused if one_head_each else local, mesh=mesh, in_specs=placed, out_specs=P("seq", "head"), check_vma=False
    )
```

```python
import functools
import math

import jax
import jax.numpy as jnp
from jax import lax
from jax.experimental import pallas as pl
from jax.experimental.pallas import tpu as pltpu
from jax.sharding import PartitionSpec as P

HEADS = 32
KV_HEADS = 8
HEAD_DIM = 128
BLOCK = 128
NT = (((1,), (1,)), ((), ()))
NN = (((1,), (0,)), ((), ()))


def dot(a, b, dims):
    return lax.dot_general(a, b, dims, preferred_element_type=jnp.float32)


def fused_kernel(
    n_seq, n_head, x_hbm, wq_hbm, wk_hbm, wv_hbm, wo_hbm, seg, out,
    xs, w, wo, acc, qs, kv, high, total, mixed, att, away, arrived, kept, sent, landed,
    x_sem, w_sem, wo_sem, x_send, x_recv, kv_send, kv_recv,
    core_send, core_recv, chip_send, chip_recv, ready,
):
    s = lax.axis_index("seq")
    h = lax.axis_index("head")
    chips = n_head // 2
    rows, cols = x_hbm.shape
    q_rows = wq_hbm.shape[0]
    dim = wk_hbm.shape[0]
    heads = q_rows // dim
    scale = 1.0 / math.sqrt(dim)

    def flipped(index):
        return index + 1 - 2 * (index % 2)

    def peer(d):
        index, bit = h, 2
        while bit < n_head:
            if 2 * d & bit:
                index = index + bit - 2 * bit * (index // bit % 2)
            bit *= 2
        return index

    def columns(owner):
        return pl.ds(pl.multiple_of(owner * cols, cols), cols)

    other = flipped(h)

    own_x = pltpu.make_async_copy(x_hbm, xs.at[h], x_sem)
    own_x.start()
    owners = []
    for d in range(chips):
        owners += [peer(d), flipped(peer(d))]
    loads = []
    for i, owner in enumerate(owners):
        chunk = []
        for j, (ref, first) in enumerate(((wk_hbm, 0), (wv_hbm, dim), (wq_hbm, 2 * dim))):
            copy = pltpu.make_async_copy(
                ref.at[:, columns(owner)],
                w.at[pl.ds(first, ref.shape[0]), columns(owner)],
                w_sem.at[i, j],
            )
            copy.start()
            chunk.append(copy)
        loads.append(chunk)
    load_wo = pltpu.make_async_copy(wo_hbm, wo, wo_sem)
    load_wo.start()

    barrier = pltpu.get_barrier_semaphore()
    for near in (other, peer(1), peer(2)):
        pl.semaphore_signal(barrier, inc=1, device_id={"head": near})

    @pl.when(s > 0)
    def _():
        pl.semaphore_signal(barrier, inc=1, device_id={"seq": s - 1})

    @pl.when(s + 1 < n_seq)
    def _():
        pl.semaphore_signal(barrier, inc=1, device_id={"seq": s + 1})

    before = (s + n_seq - 1) // n_seq
    after = (2 * n_seq - 2 - s) // n_seq
    pl.semaphore_wait(barrier, 3 + before + after)

    def tell(k):
        @pl.when((s > 0) & (s + k < n_seq))
        def _():
            pl.semaphore_signal(ready.at[k], inc=1, device_id={"seq": s - 1})

    def heard(k):
        @pl.when(s + k + 1 < n_seq)
        def _():
            pl.semaphore_wait(ready.at[k], 1)

    half = rows // 2
    sends = []

    def x_copy(owner, part, to, source=None):
        place = pl.ds(part * half, half)
        slot = xs.at[owner, place]
        return pltpu.make_async_remote_copy(
            src_ref=slot if source is None else source.at[place], dst_ref=slot,
            send_sem=x_send.at[len(sends) % x_send.shape[0]],
            recv_sem=x_recv.at[owner, part], device_id={"head": to},
        )

    def give(copy):
        copy.start()
        sends.append(copy)

    def got(owner, *parts):
        for part in parts:
            x_copy(owner, part, other).wait_recv()

    give(x_copy(h, 0, peer(1), x_hbm))
    give(x_copy(h, 1, peer(2), x_hbm))
    give(x_copy(h, 1, peer(1), x_hbm))
    give(x_copy(h, 0, peer(2), x_hbm))
    give(x_copy(h, 0, other, x_hbm))
    give(x_copy(h, 1, other, x_hbm))
    if n_seq > 2:
        tell(1)

    def multiply(i, part):
        owner = owners[i]
        product = dot(xs[owner], w[part, columns(owner)], NT)
        if i == 0:
            acc[:, part] = product
        else:
            acc[:, part] += product

    def loaded(*chunks):
        for i in chunks:
            for copy in loads[i]:
                copy.wait()

    whole = slice(0, 2 * dim + q_rows)
    memory = slice(0, 2 * dim)
    heads_part = slice(2 * dim, 2 * dim + q_rows)
    own_x.wait()
    loaded(0)
    multiply(0, whole)
    got(owners[1], 0, 1)
    loaded(1)
    multiply(1, whole)
    got(peer(1), 0)
    give(x_copy(peer(1), 0, peer(2)))
    got(peer(2), 1)
    give(x_copy(peer(2), 1, peer(1)))
    give(x_copy(peer(1), 0, other))
    give(x_copy(peer(2), 1, other))
    got(peer(1), 1)
    give(x_copy(peer(1), 1, other))
    got(peer(2), 0)
    give(x_copy(peer(2), 0, other))
    for k in range(1, n_seq - 1):
        heard(k)
        if k + 1 < n_seq - 1:
            tell(k + 1)
    for i in (2, 4):
        loaded(i)
        multiply(i, whole)
    for i in (3, 5):
        got(owners[i], 0, 1)
        loaded(i)
        multiply(i, whole)
    for part in (0, 1):
        got(peer(3), part)
        give(x_copy(peer(3), part, other))
    loaded(6, 7)
    multiply(6, memory)
    got(owners[7], 0, 1)
    multiply(7, memory)
    kv[s] = acc[:, memory].astype(jnp.bfloat16)

    def kv_copy(section, slot, to):
        return pltpu.make_async_remote_copy(
            src_ref=kv.at[section], dst_ref=kv.at[section], send_sem=kv_send.at[slot],
            recv_sem=kv_recv.at[section], device_id={"seq": to},
        )

    for j in range(n_seq - 1, 0, -1):
        @pl.when(s + j < n_seq)
        def _():
            kv_copy(s, j, s + j).start()

    multiply(6, heads_part)
    multiply(7, heads_part)
    for g in range(heads):
        qs[g * rows:(g + 1) * rows, :] = acc[:, (2 + g) * dim:(3 + g) * dim].astype(jnp.bfloat16)

    def section_segments(section):
        line = seg[:, pl.ds(pl.multiple_of(section * rows, rows), rows)]
        return jnp.broadcast_to(line, (rows, rows))

    row_segment = section_segments(s).T

    def section_scores(section, allowed):
        scores = dot(qs[...], kv[section, :, :dim], NT) * scale
        return jnp.where(jnp.concatenate([allowed] * heads, 0), scores, -1e30)

    def weighted(section, powers):
        return dot(powers.astype(jnp.bfloat16), kv[section, :, dim:], NN)

    at_row = lax.broadcasted_iota(jnp.int32, (rows, rows), 0)
    at_col = lax.broadcasted_iota(jnp.int32, (rows, rows), 1)
    scores = section_scores(s, (row_segment == section_segments(s)) & (at_col <= at_row))
    first_high = jnp.max(scores, axis=1, keepdims=True)
    powers = jnp.exp(scores - first_high)
    high[...] = first_high
    total[...] = jnp.sum(powers, axis=1, keepdims=True)
    mixed[...] = weighted(s, powers)

    for j in range(1, n_seq):
        @pl.when(s >= j)
        def _():
            section = s - j
            kv_copy(section, 0, (s + 1) % n_seq).wait_recv()
            scores = section_scores(section, row_segment == section_segments(section))
            old = high[...]
            new = jnp.maximum(old, jnp.max(scores, axis=1, keepdims=True))
            shrink = jnp.exp(old - new)
            powers = jnp.exp(scores - new)
            high[...] = new
            total[...] = total[...] * shrink + jnp.sum(powers, axis=1, keepdims=True)
            mixed[...] = mixed[...] * shrink + weighted(section, powers)

    for g in range(heads):
        part = slice(g * rows, (g + 1) * rows)
        att[:, g * dim:(g + 1) * dim] = (mixed[part, :] / total[part, :]).astype(jnp.bfloat16)

    load_wo.wait()

    def core_copy(d):
        return pltpu.make_async_remote_copy(
            src_ref=away.at[d], dst_ref=arrived.at[d], send_sem=core_send.at[d],
            recv_sem=core_recv.at[d], device_id={"head": other},
        )

    def chip_copy(d, part, through):
        place = pl.ds(part * half, half)
        return pltpu.make_async_remote_copy(
            src_ref=sent.at[d, place], dst_ref=landed.at[d, place],
            send_sem=chip_send.at[d, part], recv_sem=chip_recv.at[d, part],
            device_id={"head": peer(through)},
        )

    def project(d):
        away[d] = dot(att[...], wo[:, columns(flipped(peer(d)))], NN).astype(jnp.bfloat16)
        give(core_copy(d))
        kept[d] = dot(att[...], wo[:, columns(peer(d))], NN)

    def both_cores(d, part):
        place = slice(part * half, (part + 1) * half)
        return kept[d, place] + arrived[d, place].astype(jnp.float32)

    def pass_on(d, part, through, extra=None):
        value = both_cores(d, part)
        if extra is not None:
            value = value + extra
        sent[d, part * half:(part + 1) * half] = value.astype(jnp.bfloat16)
        give(chip_copy(d, part, through))

    def relayed(part, through):
        chip_copy(3, part, through).wait_recv()
        return landed[3, part * half:(part + 1) * half].astype(jnp.float32)

    project(3)
    project(1)
    core_copy(3).wait_recv()
    pass_on(3, 0, 1)
    pass_on(3, 1, 2)
    project(2)
    core_copy(1).wait_recv()
    pass_on(1, 0, 1)
    project(0)
    core_copy(2).wait_recv()
    pass_on(2, 1, 2)
    pass_on(2, 0, 2, relayed(0, 1))
    pass_on(1, 1, 1, relayed(1, 2))
    core_copy(0).wait_recv()
    for part in (0, 1):
        result = both_cores(0, part)
        for d in (1, 2):
            chip_copy(d, part, d).wait_recv()
            result = result + landed[d, part * half:(part + 1) * half].astype(jnp.float32)
        out[part * half:(part + 1) * half, :] = result.astype(jnp.bfloat16)

    for copy in sends:
        copy.wait_send()
    for j in range(1, n_seq):
        @pl.when(s + j < n_seq)
        def _():
            kv_copy(s, j, s + j).wait_send()


def fused(tokens, query_weight, key_weight, value_weight, output_weight, segments):
    n_seq, n_head = lax.axis_size("seq"), lax.axis_size("head")
    rows, cols = tokens.shape
    chips = n_head // 2
    q_rows, width = query_weight.shape
    dim = key_weight.shape[0]
    stacked = q_rows // dim * rows
    bf16, f32 = jnp.bfloat16, jnp.float32
    dma = pltpu.SemaphoreType.DMA
    flops = 2 * rows * width * (2 * q_rows + 2 * dim)
    return pl.pallas_call(
        functools.partial(fused_kernel, n_seq, n_head),
        out_shape=jax.ShapeDtypeStruct((rows, cols), bf16),
        in_specs=[pl.BlockSpec(memory_space=pltpu.HBM)] * 5
        + [pl.BlockSpec(memory_space=pltpu.VMEM)],
        out_specs=pl.BlockSpec(memory_space=pltpu.VMEM),
        scratch_shapes=[
            pltpu.VMEM((n_head, rows, cols), bf16),
            pltpu.VMEM((2 * dim + q_rows, width), bf16),
            pltpu.VMEM(output_weight.shape, bf16),
            pltpu.VMEM((rows, 2 * dim + q_rows), f32),
            pltpu.VMEM((stacked, dim), bf16),
            pltpu.VMEM((n_seq, rows, 2 * dim), bf16),
            pltpu.VMEM((stacked, 1), f32),
            pltpu.VMEM((stacked, 1), f32),
            pltpu.VMEM((stacked, dim), f32),
            pltpu.VMEM((rows, q_rows), bf16),
            pltpu.VMEM((chips, rows, cols), bf16),
            pltpu.VMEM((chips, rows, cols), bf16),
            pltpu.VMEM((chips, rows, cols), f32),
            pltpu.VMEM((chips, rows, cols), bf16),
            pltpu.VMEM((chips, rows, cols), bf16),
            dma, dma((n_head, 3)), dma,
            dma((14,)), dma((n_head, 2)),
            dma((n_seq,)), dma((n_seq,)),
            dma((chips,)), dma((chips,)), dma((chips, 2)), dma((chips, 2)),
            pltpu.SemaphoreType.REGULAR((n_seq,)),
        ],
        compiler_params=pltpu.CompilerParams(
            collective_id=0, has_side_effects=True, vmem_limit_bytes=56 * 2**20
        ),
        cost_estimate=pl.CostEstimate(
            flops=flops, bytes_accessed=2 * width * (2 * q_rows + 2 * dim), transcendentals=0
        ),
    )(tokens, query_weight, key_weight, value_weight, output_weight, segments.reshape(1, -1))


def swapped(block, axis, apart):
    count = lax.axis_size(axis)
    route = []
    for low in range(count):
        high = low | 1 << apart
        if high != low and high < count:
            route += [(low, high), (high, low)]
    return lax.ppermute(block, axis, route)


def trade_partner(block, bit):
    return swapped(block, "head", bit)


def collect(block, place, bit_list, dim):
    for bit in bit_list:
        flag = place >> bit & 1
        other = trade_partner(block, bit)
        block = jnp.where(
            flag == 0, jnp.concatenate([block, other], dim), jnp.concatenate([other, block], dim)
        )
    return block


def local(tokens, query_weight, key_weight, value_weight, output_weight, segments):
    n_head = lax.axis_size("head")
    split = max(1, 2 * n_head // HEADS)
    groups = n_head // split
    pair_span = n_head // KV_HEADS
    place = lax.axis_index("head")
    seq_place = lax.axis_index("seq")
    local_rows = tokens.shape[0]
    local_cols = tokens.shape[1]
    section = local_rows // split
    piece = section // groups
    split_bits = list(range(split.bit_length() - 1))
    group_bits = list(range(split.bit_length() - 1, n_head.bit_length() - 1))
    span_bits = list(range(pair_span.bit_length() - 1))
    ordered = (
        tokens.reshape(split, groups, piece, local_cols)
        .transpose(1, 0, 2, 3)
        .reshape(n_head * piece, local_cols)
    )
    arrived = lax.all_to_all(ordered, "head", split_axis=0, concat_axis=1, tiled=True)
    rows_here = collect(arrived, place, group_bits, 0)
    head_rows = collect(jnp.stack([query_weight, output_weight]), place, split_bits, 1)
    pair_rows = collect(jnp.stack([key_weight, value_weight]), place, span_bits, 1)
    queries = lax.dot_general(
        rows_here, head_rows[0], (((1,), (1,)), ((), ())), preferred_element_type=jnp.float32
    ).astype(jnp.bfloat16)
    memory_local = jnp.einsum(
        "khd,rd->khr", pair_rows, rows_here, preferred_element_type=jnp.float32
    ).astype(jnp.bfloat16)
    spread = lax.all_gather(memory_local[:, :, None, :], "seq", axis=2, tiled=True)
    memory_all = collect(spread, place, split_bits, 3).reshape(2, HEAD_DIM, -1)
    head_dim = HEAD_DIM
    heads_here = queries.shape[1] // head_dim
    first_row = seq_place * local_rows + place % split * section
    query_position = first_row + lax.iota(jnp.int32, section)
    query_segment = lax.dynamic_slice_in_dim(segments, first_row, section, 0)
    doc_start = jnp.sum((segments < query_segment[0]).astype(jnp.int32))
    first_tile = doc_start // BLOCK
    last_tile = (first_row + section - 1) // BLOCK
    grouped = queries.reshape(section, 1, heads_here, head_dim)
    scale = 1.0 / math.sqrt(head_dim)
    key_rows = memory_all[0]
    value_rows = memory_all[1]

    def visit_tile(tile, carry):
        highest, totals, accum = carry
        begin = tile * BLOCK
        key_tile = lax.dynamic_slice_in_dim(key_rows, begin, BLOCK, 1).reshape(1, head_dim, BLOCK)
        value_tile = lax.dynamic_slice_in_dim(value_rows, begin, BLOCK, 1).reshape(
            1, head_dim, BLOCK
        )
        key_segment = lax.dynamic_slice_in_dim(segments, begin, BLOCK, 0)
        key_position = begin + lax.iota(jnp.int32, BLOCK)
        allowed = (query_segment[:, None] == key_segment[None, :]) & (
            key_position[None, :] <= query_position[:, None]
        )
        scores = (
            jnp.einsum("rkgd,kdb->kgrb", grouped, key_tile, preferred_element_type=jnp.float32)
            * scale
        )
        scores = jnp.where(allowed, scores, -1e30)
        new_highest = jnp.maximum(highest, jnp.max(scores, axis=3))
        shrink = jnp.exp(highest - new_highest)
        powers = jnp.where(allowed, jnp.exp(scores - new_highest[..., None]), 0.0)
        totals = totals * shrink + jnp.sum(powers, axis=3)
        update = jnp.einsum(
            "kgrb,kdb->kgrd",
            powers.astype(jnp.bfloat16),
            value_tile,
            preferred_element_type=jnp.float32,
        )
        accum = accum * shrink[..., None] + update
        return (new_highest, totals, accum)

    start_high = jnp.full((1, heads_here, section), -1e30, jnp.float32)
    start_total = jnp.zeros((1, heads_here, section), jnp.float32)
    start_accum = jnp.zeros((1, heads_here, section, head_dim), jnp.float32)
    highest, totals, accum = lax.fori_loop(
        first_tile, last_tile + 1, visit_tile, (start_high, start_total, start_accum)
    )
    attended = (
        (accum / totals[..., None])
        .transpose(2, 0, 1, 3)
        .reshape(section, heads_here * head_dim)
        .astype(jnp.bfloat16)
    )
    pairs_here = heads_here // 2
    partial_value = jnp.einsum(
        "rpk,pkd->prd",
        attended.reshape(section, pairs_here, 2 * head_dim),
        head_rows[1].reshape(pairs_here, 2 * head_dim, -1),
        preferred_element_type=jnp.float32,
    ).astype(jnp.bfloat16)
    returned = lax.all_to_all(partial_value, "head", split_axis=2, concat_axis=0, tiled=True)
    summed = (
        returned.astype(jnp.float32)
        .reshape(groups, split, pairs_here, section, -1)
        .sum(axis=(0, 2))
    )
    return summed.reshape(split * section, -1).astype(jnp.bfloat16)


def solution(mesh):
    placed = (
        P("seq", "head"),
        P("head", None),
        P("head", None),
        P("head", None),
        P("head", None),
        P(),
    )
    one_head_each = mesh.shape["head"] == KV_HEADS
    return jax.shard_map(
        fused if one_head_each else local, mesh=mesh, in_specs=placed, out_specs=P("seq", "head"), check_vma=False
    )
```

```python
import functools
import math

import jax
import jax.numpy as jnp
from jax import lax
from jax.experimental import pallas as pl
from jax.experimental.pallas import tpu as pltpu
from jax.sharding import PartitionSpec as P

HEADS = 32
KV_HEADS = 8
HEAD_DIM = 128
BLOCK = 128
NT = (((1,), (1,)), ((), ()))
NN = (((1,), (0,)), ((), ()))


def dot(a, b, dims):
    return lax.dot_general(a, b, dims, preferred_element_type=jnp.float32)


def fused_kernel(
    n_seq, n_head, x_hbm, wq_hbm, wk_hbm, wv_hbm, wo_hbm, seg, out,
    xs, w, wo, acc, qs, kv, high, total, mixed, att, away, arrived, kept, sent, landed,
    x_sem, w_sem, wo_sem, x_send, x_recv, kv_send, kv_recv,
    core_send, core_recv, chip_send, chip_recv, ready,
):
    s = lax.axis_index("seq")
    h = lax.axis_index("head")
    chips = n_head // 2
    rows, cols = x_hbm.shape
    q_rows = wq_hbm.shape[0]
    dim = wk_hbm.shape[0]
    heads = q_rows // dim
    scale = 1.0 / math.sqrt(dim)

    def flipped(index):
        return index + 1 - 2 * (index % 2)

    def peer(d):
        index, bit = h, 2
        while bit < n_head:
            if 2 * d & bit:
                index = index + bit - 2 * bit * (index // bit % 2)
            bit *= 2
        return index

    def columns(owner):
        return pl.ds(pl.multiple_of(owner * cols, cols), cols)

    other = flipped(h)

    own_x = pltpu.make_async_copy(x_hbm, xs.at[h], x_sem)
    own_x.start()
    barrier = pltpu.get_barrier_semaphore()
    for near in (other, peer(1), peer(2)):
        pl.semaphore_signal(barrier, inc=1, device_id={"head": near})

    @pl.when(s > 0)
    def _():
        pl.semaphore_signal(barrier, inc=1, device_id={"seq": s - 1})

    @pl.when(s + 1 < n_seq)
    def _():
        pl.semaphore_signal(barrier, inc=1, device_id={"seq": s + 1})

    owners = []
    for d in range(chips):
        owners += [peer(d), flipped(peer(d))]
    loads = []
    for i, owner in enumerate(owners):
        chunk = []
        for j, (ref, first) in enumerate(((wk_hbm, 0), (wv_hbm, dim), (wq_hbm, 2 * dim))):
            copy = pltpu.make_async_copy(
                ref.at[:, columns(owner)],
                w.at[pl.ds(first, ref.shape[0]), columns(owner)],
                w_sem.at[i, j],
            )
            copy.start()
            chunk.append(copy)
        loads.append(chunk)
    load_wo = pltpu.make_async_copy(wo_hbm, wo, wo_sem)
    load_wo.start()

    before = (s + n_seq - 1) // n_seq
    after = (2 * n_seq - 2 - s) // n_seq
    pl.semaphore_wait(barrier, 3 + before + after)

    def tell(k):
        @pl.when((s > 0) & (s + k < n_seq))
        def _():
            pl.semaphore_signal(ready.at[k], inc=1, device_id={"seq": s - 1})

    def heard(k):
        @pl.when(s + k + 1 < n_seq)
        def _():
            pl.semaphore_wait(ready.at[k], 1)

    half = rows // 2
    sends = []

    def x_copy(owner, part, to):
        place = pl.ds(part * half, half)
        slot = xs.at[owner, place]
        return pltpu.make_async_remote_copy(
            src_ref=slot, dst_ref=slot,
            send_sem=x_send.at[len(sends) % x_send.shape[0]],
            recv_sem=x_recv.at[owner, part], device_id={"head": to},
        )

    def give(copy):
        copy.start()
        sends.append(copy)

    def got(owner, *parts):
        for part in parts:
            x_copy(owner, part, other).wait_recv()

    own_x.wait()
    give(x_copy(h, 0, peer(1)))
    give(x_copy(h, 1, peer(2)))
    give(x_copy(h, 1, peer(1)))
    give(x_copy(h, 0, peer(2)))
    give(x_copy(h, 0, other))
    give(x_copy(h, 1, other))
    if n_seq > 2:
        tell(1)

    def multiply(i, part):
        owner = owners[i]
        product = dot(xs[owner], w[part, columns(owner)], NT)
        if i == 0:
            acc[:, part] = product
        else:
            acc[:, part] += product

    def loaded(*chunks):
        for i in chunks:
            for copy in loads[i]:
                copy.wait()

    whole = slice(0, 2 * dim + q_rows)
    memory = slice(0, 2 * dim)
    heads_part = slice(2 * dim, 2 * dim + q_rows)
    loaded(0)
    multiply(0, whole)
    got(owners[1], 0, 1)
    loaded(1)
    multiply(1, whole)
    got(peer(1), 0)
    give(x_copy(peer(1), 0, peer(2)))
    got(peer(2), 1)
    give(x_copy(peer(2), 1, peer(1)))
    give(x_copy(peer(1), 0, other))
    give(x_copy(peer(2), 1, other))
    got(peer(1), 1)
    give(x_copy(peer(1), 1, other))
    got(peer(2), 0)
    give(x_copy(peer(2), 0, other))
    for i in (2, 4):
        loaded(i)
        multiply(i, whole)
    for i in (3, 5):
        got(owners[i], 0, 1)
        loaded(i)
        multiply(i, whole)
    if n_seq > 2:
        heard(1)
    if n_seq > 3:
        tell(2)
    for part in (0, 1):
        got(peer(3), part)
        give(x_copy(peer(3), part, other))
    loaded(6, 7)
    multiply(6, memory)
    got(owners[7], 0, 1)
    multiply(7, memory)
    kv[s] = acc[:, memory].astype(jnp.bfloat16)

    def kv_copy(section, slot, to):
        return pltpu.make_async_remote_copy(
            src_ref=kv.at[section], dst_ref=kv.at[section], send_sem=kv_send.at[slot],
            recv_sem=kv_recv.at[section], device_id={"seq": to},
        )

    for k in range(2, n_seq - 1):
        heard(k)
        if k + 1 < n_seq - 1:
            tell(k + 1)
    for j in range(1, n_seq):
        @pl.when(s + j < n_seq)
        def _():
            kv_copy(s, j, s + j).start()

    multiply(6, heads_part)
    multiply(7, heads_part)
    for g in range(heads):
        qs[g * rows:(g + 1) * rows, :] = acc[:, (2 + g) * dim:(3 + g) * dim].astype(jnp.bfloat16)

    def section_segments(section):
        line = seg[:, pl.ds(pl.multiple_of(section * rows, rows), rows)]
        return jnp.broadcast_to(line, (rows, rows))

    row_segment = section_segments(s).T

    def section_scores(section, allowed):
        scores = dot(qs[...], kv[section, :, :dim], NT) * scale
        return jnp.where(jnp.concatenate([allowed] * heads, 0), scores, -1e30)

    def weighted(section, powers):
        return dot(powers.astype(jnp.bfloat16), kv[section, :, dim:], NN)

    at_row = lax.broadcasted_iota(jnp.int32, (rows, rows), 0)
    at_col = lax.broadcasted_iota(jnp.int32, (rows, rows), 1)
    scores = section_scores(s, (row_segment == section_segments(s)) & (at_col <= at_row))
    first_high = jnp.max(scores, axis=1, keepdims=True)
    powers = jnp.exp(scores - first_high)
    high[...] = first_high
    total[...] = jnp.sum(powers, axis=1, keepdims=True)
    mixed[...] = weighted(s, powers)

    for j in range(1, n_seq):
        @pl.when(s >= j)
        def _():
            section = s - j
            kv_copy(section, 0, (s + 1) % n_seq).wait_recv()
            scores = section_scores(section, row_segment == section_segments(section))
            old = high[...]
            new = jnp.maximum(old, jnp.max(scores, axis=1, keepdims=True))
            shrink = jnp.exp(old - new)
            powers = jnp.exp(scores - new)
            high[...] = new
            total[...] = total[...] * shrink + jnp.sum(powers, axis=1, keepdims=True)
            mixed[...] = mixed[...] * shrink + weighted(section, powers)

    for g in range(heads):
        part = slice(g * rows, (g + 1) * rows)
        att[:, g * dim:(g + 1) * dim] = (mixed[part, :] / total[part, :]).astype(jnp.bfloat16)

    load_wo.wait()

    def core_copy(d):
        return pltpu.make_async_remote_copy(
            src_ref=away.at[d], dst_ref=arrived.at[d], send_sem=core_send.at[d],
            recv_sem=core_recv.at[d], device_id={"head": other},
        )

    def chip_copy(d, part, through):
        place = pl.ds(part * half, half)
        return pltpu.make_async_remote_copy(
            src_ref=sent.at[d, place], dst_ref=landed.at[d, place],
            send_sem=chip_send.at[d, part], recv_sem=chip_recv.at[d, part],
            device_id={"head": peer(through)},
        )

    def project(d):
        away[d] = dot(att[...], wo[:, columns(flipped(peer(d)))], NN).astype(jnp.bfloat16)
        give(core_copy(d))
        kept[d] = dot(att[...], wo[:, columns(peer(d))], NN)

    def both_cores(d, part):
        place = slice(part * half, (part + 1) * half)
        return kept[d, place] + arrived[d, place].astype(jnp.float32)

    def pass_on(d, part, through, extra=None):
        value = both_cores(d, part)
        if extra is not None:
            value = value + extra
        sent[d, part * half:(part + 1) * half] = value.astype(jnp.bfloat16)
        give(chip_copy(d, part, through))

    def relayed(part, through):
        chip_copy(3, part, through).wait_recv()
        return landed[3, part * half:(part + 1) * half].astype(jnp.float32)

    project(3)
    project(1)
    core_copy(3).wait_recv()
    pass_on(3, 0, 1)
    pass_on(3, 1, 2)
    project(2)
    core_copy(1).wait_recv()
    pass_on(1, 0, 1)
    project(0)
    core_copy(2).wait_recv()
    pass_on(2, 1, 2)
    pass_on(2, 0, 2, relayed(0, 1))
    pass_on(1, 1, 1, relayed(1, 2))
    core_copy(0).wait_recv()
    for part in (0, 1):
        result = both_cores(0, part)
        for d in (1, 2):
            chip_copy(d, part, d).wait_recv()
            result = result + landed[d, part * half:(part + 1) * half].astype(jnp.float32)
        out[part * half:(part + 1) * half, :] = result.astype(jnp.bfloat16)

    for copy in sends:
        copy.wait_send()
    for j in range(1, n_seq):
        @pl.when(s + j < n_seq)
        def _():
            kv_copy(s, j, s + j).wait_send()


def fused(tokens, query_weight, key_weight, value_weight, output_weight, segments):
    n_seq, n_head = lax.axis_size("seq"), lax.axis_size("head")
    rows, cols = tokens.shape
    chips = n_head // 2
    q_rows, width = query_weight.shape
    dim = key_weight.shape[0]
    stacked = q_rows // dim * rows
    bf16, f32 = jnp.bfloat16, jnp.float32
    dma = pltpu.SemaphoreType.DMA
    flops = 2 * rows * width * (2 * q_rows + 2 * dim)
    return pl.pallas_call(
        functools.partial(fused_kernel, n_seq, n_head),
        out_shape=jax.ShapeDtypeStruct((rows, cols), bf16),
        in_specs=[pl.BlockSpec(memory_space=pltpu.HBM)] * 5
        + [pl.BlockSpec(memory_space=pltpu.VMEM)],
        out_specs=pl.BlockSpec(memory_space=pltpu.VMEM),
        scratch_shapes=[
            pltpu.VMEM((n_head, rows, cols), bf16),
            pltpu.VMEM((2 * dim + q_rows, width), bf16),
            pltpu.VMEM(output_weight.shape, bf16),
            pltpu.VMEM((rows, 2 * dim + q_rows), f32),
            pltpu.VMEM((stacked, dim), bf16),
            pltpu.VMEM((n_seq, rows, 2 * dim), bf16),
            pltpu.VMEM((stacked, 1), f32),
            pltpu.VMEM((stacked, 1), f32),
            pltpu.VMEM((stacked, dim), f32),
            pltpu.VMEM((rows, q_rows), bf16),
            pltpu.VMEM((chips, rows, cols), bf16),
            pltpu.VMEM((chips, rows, cols), bf16),
            pltpu.VMEM((chips, rows, cols), f32),
            pltpu.VMEM((chips, rows, cols), bf16),
            pltpu.VMEM((chips, rows, cols), bf16),
            dma, dma((n_head, 3)), dma,
            dma((14,)), dma((n_head, 2)),
            dma((n_seq,)), dma((n_seq,)),
            dma((chips,)), dma((chips,)), dma((chips, 2)), dma((chips, 2)),
            pltpu.SemaphoreType.REGULAR((n_seq,)),
        ],
        compiler_params=pltpu.CompilerParams(
            collective_id=0, has_side_effects=True, vmem_limit_bytes=56 * 2**20
        ),
        cost_estimate=pl.CostEstimate(
            flops=flops, bytes_accessed=2 * width * (2 * q_rows + 2 * dim), transcendentals=0
        ),
    )(tokens, query_weight, key_weight, value_weight, output_weight, segments.reshape(1, -1))


def swapped(block, axis, apart):
    count = lax.axis_size(axis)
    route = []
    for low in range(count):
        high = low | 1 << apart
        if high != low and high < count:
            route += [(low, high), (high, low)]
    return lax.ppermute(block, axis, route)


def trade_partner(block, bit):
    return swapped(block, "head", bit)


def collect(block, place, bit_list, dim):
    for bit in bit_list:
        flag = place >> bit & 1
        other = trade_partner(block, bit)
        block = jnp.where(
            flag == 0, jnp.concatenate([block, other], dim), jnp.concatenate([other, block], dim)
        )
    return block


def local(tokens, query_weight, key_weight, value_weight, output_weight, segments):
    n_head = lax.axis_size("head")
    split = max(1, 2 * n_head // HEADS)
    groups = n_head // split
    pair_span = n_head // KV_HEADS
    place = lax.axis_index("head")
    seq_place = lax.axis_index("seq")
    local_rows = tokens.shape[0]
    local_cols = tokens.shape[1]
    section = local_rows // split
    piece = section // groups
    split_bits = list(range(split.bit_length() - 1))
    group_bits = list(range(split.bit_length() - 1, n_head.bit_length() - 1))
    span_bits = list(range(pair_span.bit_length() - 1))
    ordered = (
        tokens.reshape(split, groups, piece, local_cols)
        .transpose(1, 0, 2, 3)
        .reshape(n_head * piece, local_cols)
    )
    arrived = lax.all_to_all(ordered, "head", split_axis=0, concat_axis=1, tiled=True)
    rows_here = collect(arrived, place, group_bits, 0)
    head_rows = collect(jnp.stack([query_weight, output_weight]), place, split_bits, 1)
    pair_rows = collect(jnp.stack([key_weight, value_weight]), place, span_bits, 1)
    queries = lax.dot_general(
        rows_here, head_rows[0], (((1,), (1,)), ((), ())), preferred_element_type=jnp.float32
    ).astype(jnp.bfloat16)
    memory_local = jnp.einsum(
        "khd,rd->khr", pair_rows, rows_here, preferred_element_type=jnp.float32
    ).astype(jnp.bfloat16)
    spread = lax.all_gather(memory_local[:, :, None, :], "seq", axis=2, tiled=True)
    memory_all = collect(spread, place, split_bits, 3).reshape(2, HEAD_DIM, -1)
    head_dim = HEAD_DIM
    heads_here = queries.shape[1] // head_dim
    first_row = seq_place * local_rows + place % split * section
    query_position = first_row + lax.iota(jnp.int32, section)
    query_segment = lax.dynamic_slice_in_dim(segments, first_row, section, 0)
    doc_start = jnp.sum((segments < query_segment[0]).astype(jnp.int32))
    first_tile = doc_start // BLOCK
    last_tile = (first_row + section - 1) // BLOCK
    grouped = queries.reshape(section, 1, heads_here, head_dim)
    scale = 1.0 / math.sqrt(head_dim)
    key_rows = memory_all[0]
    value_rows = memory_all[1]

    def visit_tile(tile, carry):
        highest, totals, accum = carry
        begin = tile * BLOCK
        key_tile = lax.dynamic_slice_in_dim(key_rows, begin, BLOCK, 1).reshape(1, head_dim, BLOCK)
        value_tile = lax.dynamic_slice_in_dim(value_rows, begin, BLOCK, 1).reshape(
            1, head_dim, BLOCK
        )
        key_segment = lax.dynamic_slice_in_dim(segments, begin, BLOCK, 0)
        key_position = begin + lax.iota(jnp.int32, BLOCK)
        allowed = (query_segment[:, None] == key_segment[None, :]) & (
            key_position[None, :] <= query_position[:, None]
        )
        scores = (
            jnp.einsum("rkgd,kdb->kgrb", grouped, key_tile, preferred_element_type=jnp.float32)
            * scale
        )
        scores = jnp.where(allowed, scores, -1e30)
        new_highest = jnp.maximum(highest, jnp.max(scores, axis=3))
        shrink = jnp.exp(highest - new_highest)
        powers = jnp.where(allowed, jnp.exp(scores - new_highest[..., None]), 0.0)
        totals = totals * shrink + jnp.sum(powers, axis=3)
        update = jnp.einsum(
            "kgrb,kdb->kgrd",
            powers.astype(jnp.bfloat16),
            value_tile,
            preferred_element_type=jnp.float32,
        )
        accum = accum * shrink[..., None] + update
        return (new_highest, totals, accum)

    start_high = jnp.full((1, heads_here, section), -1e30, jnp.float32)
    start_total = jnp.zeros((1, heads_here, section), jnp.float32)
    start_accum = jnp.zeros((1, heads_here, section, head_dim), jnp.float32)
    highest, totals, accum = lax.fori_loop(
        first_tile, last_tile + 1, visit_tile, (start_high, start_total, start_accum)
    )
    attended = (
        (accum / totals[..., None])
        .transpose(2, 0, 1, 3)
        .reshape(section, heads_here * head_dim)
        .astype(jnp.bfloat16)
    )
    pairs_here = heads_here // 2
    partial_value = jnp.einsum(
        "rpk,pkd->prd",
        attended.reshape(section, pairs_here, 2 * head_dim),
        head_rows[1].reshape(pairs_here, 2 * head_dim, -1),
        preferred_element_type=jnp.float32,
    ).astype(jnp.bfloat16)
    returned = lax.all_to_all(partial_value, "head", split_axis=2, concat_axis=0, tiled=True)
    summed = (
        returned.astype(jnp.float32)
        .reshape(groups, split, pairs_here, section, -1)
        .sum(axis=(0, 2))
    )
    return summed.reshape(split * section, -1).astype(jnp.bfloat16)


def solution(mesh):
    placed = (
        P("seq", "head"),
        P("head", None),
        P("head", None),
        P("head", None),
        P("head", None),
        P(),
    )
    one_head_each = mesh.shape["head"] == KV_HEADS
    return jax.shard_map(
        fused if one_head_each else local, mesh=mesh, in_specs=placed, out_specs=P("seq", "head"), check_vma=False
    )
```
